32 devices in a mesh: grp: 2 (over x), op: 16 (over z, y, core).
Axes of the slice: x: 2, y: 2, z: 4, core: 2. Of those that a mesh axis runs over, the one named last changes fastest.
Arguments:
- wavefunction: bfloat16 [4, 2048, 256], P('grp', 'op'), parts along dimension 0, may hold values from -6 to 6
- left_ops: bfloat16 [1024, 256, 256], P(('grp', 'op')), parts along dimension 0, may hold values from -0.375 to 0.375
- right_ops: bfloat16 [1024, 256, 256], P(('grp', 'op')), parts along dimension 0, may hold values from -0.0546875 to 0.0546875
- left_index: int32 [3072], P(('grp', 'op')), parts along dimension 0, may hold values from 0 to 31
- right_index: int32 [3072], P(('grp', 'op')), parts along dimension 0, may hold values from 0 to 31
- source_block: int32 [3072], P(('grp', 'op')), parts along dimension 0, may hold values from 0 to 7
- target_block: int32 [3072], P(('grp', 'op')), parts along dimension 0, may hold values from 0 to 7
- live_count: int32 [32], P(('grp', 'op')), parts along dimension 0, may hold values from 1 to 96, as said below
Outputs:
- sigma: float32 [4, 2048, 256], P('grp', 'op'), parts along dimension 0
The draws below stay inside these ranges and needn't reach their ends.
There are 2 independent parts, one for each index of `grp`. The reference program is written for one: setup_inputs(seed, part) draws one part's arguments, and reference() takes and returns one part's arrays. A program takes and returns all parts, laid end to end along the dimension named above; each array names one. Nothing has to cross between parts.
Inputs may be any that keep to these rules, and one draw needn't show every extreme that they name: `live_count`: the live terms of an operator group occupy its first slots; in every draw one group has all 96 slots live.
All inputs are finite; a program needn't handle non-finite values.
Results may differ from the reference program's by a relative error of at most 0.003.
Values may be sent and summed in bfloat16 or wider, within the bound.
A program may use at most 128 MiB of HBM per device.

```python
import jax
import jax.numpy as jnp
from jax import lax

B = 256
NB = 8
TERM_DEV = 96
OPS_DEV = 32
TERMS = 1536
OPS = 512
N_OP = 16


def draw_live_count(key, part):
    key = jax.random.fold_in(key, 11)
    base_key, full_key = jax.random.split(key)
    counts = jax.random.randint(base_key, (N_OP,), 1, TERM_DEV // 2 + 1, dtype=jnp.int32)
    busiest = jax.random.randint(full_key, (), 0, N_OP, dtype=jnp.int32)
    places = jnp.arange(N_OP, dtype=jnp.int32)
    return jnp.where(places == busiest, jnp.int32(TERM_DEV), counts)


def touch_ends(result, own_key, least, top_value):
    longest = result.shape.index(max(result.shape))
    spots = []
    for shift in (0, 1):
        where = [jax.random.randint(jax.random.fold_in(own_key, axis), (), 0, length) for axis, length in enumerate(result.shape)]
        where[longest] = (where[longest] + shift) % result.shape[longest]
        spots.append(tuple(where))
    return result.at[spots[0]].set(least).at[spots[1]].set(top_value)


def shard_levels(rng, dims, pieces, smallest, largest):
    gain, own = 1.0, jax.random.fold_in(rng, 6)
    for dim, blocks in pieces:
        draws = jnp.exp(jax.random.uniform(jax.random.fold_in(own, dim), (blocks,), jnp.float32, smallest / len(pieces), largest / len(pieces)))
        gain = gain * jnp.repeat(draws, dims[dim] // blocks).reshape([-1 if axis == dim else 1 for axis in range(len(dims))])
    return gain


def scatter_about(rng, dims, scale, bound, cuts=(), kind=jnp.bfloat16):
    drawn = scale * jax.random.normal(rng, dims, jnp.float32)
    if cuts:
        drawn = drawn * shard_levels(rng, dims, cuts, -0.22, 0.18)
    return jnp.clip(drawn, -bound, bound).astype(kind)


def setup_inputs(seed: int = 0, part: int = 0) -> dict:
    keys = jax.random.split(jax.random.key(seed), 9)
    own_keys = jax.random.split(jax.random.fold_in(keys[8], part), 9)
    wavefunction = scatter_about(own_keys[0], (2, NB * B, B), 1.0, 6.0, ((1, 16),))
    left_ops = scatter_about(own_keys[1], (OPS, B, B), B ** -0.5, 0.375, ((0, 16),))
    right_ops = scatter_about(own_keys[2], (OPS, B, B), (B * N_OP * TERM_DEV // (4 * NB)) ** -0.5, 0.0546875, ((0, 16),))
    left_index = touch_ends(jax.random.randint(own_keys[3], (TERMS,), 0, OPS_DEV), jax.random.fold_in(own_keys[3], 1), 0, OPS_DEV - 1).astype(jnp.int32)
    right_index = touch_ends(jax.random.randint(own_keys[4], (TERMS,), 0, OPS_DEV), jax.random.fold_in(own_keys[4], 1), 0, OPS_DEV - 1).astype(jnp.int32)
    source_block = touch_ends(jax.random.randint(own_keys[5], (TERMS,), 0, NB), jax.random.fold_in(own_keys[5], 1), 0, NB - 1).astype(jnp.int32)
    target_block = touch_ends(jax.random.randint(own_keys[6], (TERMS,), 0, NB), jax.random.fold_in(own_keys[6], 1), 0, NB - 1).astype(jnp.int32)
    live_count = draw_live_count(jax.random.fold_in(jax.random.fold_in(keys[8], part), 71), part)
    return dict(wavefunction=wavefunction, left_ops=left_ops, right_ops=right_ops, left_index=left_index, right_index=right_index, source_block=source_block, target_block=target_block, live_count=live_count)


def reference(wavefunction, left_ops, right_ops, left_index, right_index, source_block, target_block, live_count):
    blocks = wavefunction.astype(jnp.float32).reshape(2, NB, B, B)
    slots = jnp.arange(TERM_DEV, dtype=jnp.int32)

    def group_terms(summed, group):
        first = (group * TERM_DEV).astype(jnp.int32)
        left_pick = lax.dynamic_slice_in_dim(left_index, first, TERM_DEV) + group * OPS_DEV
        right_pick = lax.dynamic_slice_in_dim(right_index, first, TERM_DEV) + group * OPS_DEV
        source_pick = lax.dynamic_slice_in_dim(source_block, first, TERM_DEV)
        target_pick = lax.dynamic_slice_in_dim(target_block, first, TERM_DEV)
        lefts = jnp.take(left_ops, left_pick, axis=0).astype(jnp.float32)
        rights = jnp.take(right_ops, right_pick, axis=0).astype(jnp.float32)
        picked = jnp.take(blocks, source_pick, axis=1)
        left_part = jnp.einsum('kij,vkjm->kvim', lefts, picked).astype(jnp.bfloat16)
        left_part = lax.optimization_barrier(left_part).astype(jnp.float32)
        term_part = jnp.einsum('kvim,kmn->kvin', left_part, rights)
        active = (slots < live_count[group]).astype(jnp.float32)
        term_part = term_part * active[:, None, None, None]
        return summed + jax.ops.segment_sum(term_part, target_pick, num_segments=NB), None

    start = jnp.zeros((NB, 2, B, B), jnp.float32)
    summed, _ = lax.scan(group_terms, start, jnp.arange(N_OP, dtype=jnp.int32))
    return summed.transpose(1, 0, 2, 3).reshape(2, NB * B, B)
```

```python
import functools

import jax
import jax.numpy as jnp
from jax import lax
from jax.experimental import pallas as pl
from jax.experimental.pallas import tpu as pltpu
from jax.sharding import PartitionSpec as P

MESH = pl.DeviceIdType.MESH
UNROLL = 2
SEGMENTS = 6


def plan_terms(left_index, right_index, source_block, target_block, live_count, nblocks):
    slots = left_index.shape[0]
    ids = jnp.arange(slots, dtype=jnp.int32)
    target = jnp.where(ids < live_count[0], target_block, nblocks)
    key = target * slots + ids
    rank = jnp.sum((key[None, :] < key[:, None]).astype(jnp.int32), axis=1)
    place = (rank[None, :] == ids[:, None]).astype(jnp.int32)
    rows = jnp.stack([left_index, right_index, source_block, target])
    rows = jnp.sum(rows[:, None, :] * place[None], axis=2)
    before = jnp.concatenate([jnp.full((1,), -1, jnp.int32), rows[3, :-1]])
    keep = (rows[3] == before).astype(jnp.int32)
    ends = jnp.sum((target[None, :] <= ids[:, None]).astype(jnp.int32), axis=1)
    any_term = jnp.sum((target[None, :] == ids[:, None]).astype(jnp.int32), axis=1) > 0
    return jnp.concatenate([rows[:3], jnp.stack([keep, ends, any_term.astype(jnp.int32)])])


def kernel(far, near, plan, wave, left_hbm, right_hbm, out,
           lefts, rights, psi0, psi1, hist, ended, send_c, recv_c, send_y, recv_y, send_z, recv_z,
           ops_sem, zsem, ysem, csem):
    psi = (psi0, psi1)
    rows = wave.shape[1]
    width = wave.shape[2]
    slots = plan.shape[1]
    me = lax.axis_index("op")
    c = lax.rem(me, 2)
    y = lax.rem(me // 2, near)
    z = me // (2 * near)

    def index_of(a, b, core):
        return (a * near + b) * 2 + core

    def place_of(idx):
        row = idx * rows
        return row // width, pl.ds(pl.multiple_of(lax.rem(row, width), rows), rows)

    def shift(at, by, size):
        return lax.rem(at + by + size, size)

    sibling = index_of(z, y, 1 - c)
    y_peer = [index_of(z, shift(y, d, near), c) for d in range(near)]
    z_peer = [index_of(shift(z, d, far), y, c) for d in range(far)]
    peers = [sibling] + y_peer[1:] + z_peer[1:]

    loads = [
        pltpu.make_async_copy(left_hbm, lefts, ops_sem.at[0]),
        pltpu.make_async_copy(right_hbm, rights, ops_sem.at[1]),
    ]
    for load in loads:
        load.start()
    barrier = pltpu.get_barrier_semaphore()
    for peer in peers:
        pl.semaphore_signal(barrier, inc=1, device_id={"op": peer}, device_id_type=MESH)
    for v in range(2):
        psi[v][place_of(me)] = wave[v]
    pl.semaphore_wait(barrier, len(peers))

    sent = []

    def remote(src, dst, sems, peer):
        return pltpu.make_async_remote_copy(
            src_ref=src, dst_ref=dst, send_sem=sems[0], recv_sem=sems[1],
            device_id={"op": peer}, device_id_type=MESH,
        )

    def send(src, dst, sems, peer):
        copy = remote(src, dst, sems, peer)
        copy.start()
        sent.append(copy)

    def sem_pair(array, *place):
        return array.at[(*place, 0)], array.at[(*place, 1)]

    def chunk(v, idx):
        return psi[v].at[place_of(idx)]

    def gather_copy(v, sems, idx, peer):
        send(chunk(v, idx), chunk(v, idx), sems, peer)

    def gather_wait(v, sems, idx, peer):
        remote(chunk(v, idx), chunk(v, idx), sems, peer).wait_recv()

    def source(dy, dz, core):
        return index_of(shift(z, -dz, far), shift(y, -dy, near), core)

    def spread(v, dz):
        idx = source(0, dz, c)
        for dy in range(1, near):
            gather_copy(v, sem_pair(ysem, 0, v, dy, dz), idx, y_peer[dy])
        gather_copy(v, sem_pair(csem, 0, v, 0, dz), idx, sibling)

    def gather_own(v):
        for dz in range(1, far):
            gather_copy(v, sem_pair(zsem, 0, v, dz), me, z_peer[dz])
        spread(v, 0)

    z_order = sorted(range(1, far), key=lambda d: min(d, far - d))

    def gather_far(v):
        for dz in z_order:
            gather_wait(v, sem_pair(zsem, 0, v, dz), source(0, dz, c), z_peer[dz])
            spread(v, dz)

    def gather_near(v):
        for dz in [0] + z_order:
            for dy in range(1, near):
                idx = source(dy, dz, c)
                gather_wait(v, sem_pair(ysem, 0, v, dy, dz), idx, y_peer[dy])
                gather_copy(v, sem_pair(csem, 0, v, dy, dz), idx, sibling)

    def gather_end(v):
        for dz in range(far):
            for dy in range(near):
                gather_wait(v, sem_pair(csem, 0, v, dy, dz), source(dy, dz, 1 - c), sibling)

    def terms(v, first, last):
        def body(i, carry):
            base = first + i * UNROLL
            parts = []
            for u in range(UNROLL):
                t = base + u
                block = psi[v][plan[2, t]]
                parts.append(
                    jnp.dot(lefts[plan[0, t]], block, preferred_element_type=jnp.float32)
                    .astype(jnp.bfloat16)
                )
            total = hist[base]
            for u in range(UNROLL):
                t = base + u
                total = total * plan[3, t].astype(jnp.float32) + jnp.dot(
                    parts[u], rights[plan[1, t]], preferred_element_type=jnp.float32
                )
                hist[t + 1] = total
            return carry

        lax.fori_loop(0, (last - first) // UNROLL, body, 0)

    def finish(v):
        for q in range(ended.shape[1]):
            ended[v, q] = hist[plan[4, q]] * plan[5, q].astype(jnp.float32)

    def partial(v, idx):
        return ended[(v, *place_of(idx))]

    f32 = jnp.float32
    bf16 = jnp.bfloat16

    def reduce_core(v):
        finish(v)
        for dy in list(range(1, near)) + [0]:
            for dz in z_order + [0]:
                a, b = shift(z, dz, far), shift(y, dy, near)
                send_c[v, dy, dz] = partial(v, index_of(a, b, 1 - c)).astype(bf16)
                send(send_c.at[v, dy, dz], recv_c.at[v, dy, dz], sem_pair(csem, 1, v, dy, dz), sibling)

    def core_sum(v, dy, dz):
        remote(send_c.at[v, dy, dz], recv_c.at[v, dy, dz], sem_pair(csem, 1, v, dy, dz), sibling).wait_recv()
        a, b = shift(z, dz, far), shift(y, dy, near)
        return partial(v, index_of(a, b, c)) + recv_c[v, dy, dz].astype(f32)

    def reduce_near(v):
        for dz in z_order + [0]:
            for dy in range(1, near):
                send_y[v, dy, dz] = core_sum(v, dy, dz).astype(bf16)
                send(send_y.at[v, dy, dz], recv_y.at[v, dy, dz], sem_pair(ysem, 1, v, dy, dz), y_peer[dy])

    def near_sum(v, dz):
        total = core_sum(v, 0, dz)
        for dy in range(1, near):
            remote(send_y.at[v, dy, dz], recv_y.at[v, dy, dz], sem_pair(ysem, 1, v, dy, dz), y_peer[dy]).wait_recv()
            total = total + recv_y[v, dy, dz].astype(f32)
        return total

    def reduce_far(v):
        for dz in z_order:
            send_z[v, dz] = near_sum(v, dz).astype(bf16)
            send(send_z.at[v, dz], recv_z.at[v, dz], sem_pair(zsem, 1, v, dz), z_peer[dz])
        out[v] = near_sum(v, 0)

    def reduce_end(v):
        total = out[v]
        for dz in z_order:
            remote(send_z.at[v, dz], recv_z.at[v, dz], sem_pair(zsem, 1, v, dz), z_peer[dz]).wait_recv()
            total = total + recv_z[v, dz].astype(f32)
        out[v] = total

    cuts = [slots * i // (SEGMENTS * UNROLL) * UNROLL for i in range(SEGMENTS)] + [slots]
    gather_own(0)
    hist[0] = jnp.zeros(hist.shape[1:], f32)
    gather_far(0)
    gather_own(1)
    gather_near(0)
    gather_end(0)
    for load in loads:
        load.wait()
    beside0 = {1: gather_far, 3: gather_near}
    for s in range(SEGMENTS):
        terms(0, cuts[s], cuts[s + 1])
        if s in beside0:
            beside0[s](1)
    gather_end(1)
    reduce_core(0)
    beside1 = {0: reduce_near, 3: reduce_far}
    for s in range(SEGMENTS):
        terms(1, cuts[s], cuts[s + 1])
        if s in beside1:
            beside1[s](0)
    reduce_core(1)
    reduce_near(1)
    reduce_far(1)
    reduce_end(0)
    reduce_end(1)
    for copy in sent:
        copy.wait_send()


def per_device(devices, wavefunction, left_ops, right_ops, left_index, right_index,
               source_block, target_block, live_count):
    pairs = devices // 2
    far = 1
    while far * far < pairs:
        far *= 2
    near = pairs // far
    vectors, rows, width = wavefunction.shape
    nblocks = devices * rows // width
    slots = left_index.shape[0]
    plan = plan_terms(left_index, right_index, source_block, target_block, live_count, nblocks)
    sems = pltpu.SemaphoreType.DMA
    bf16 = jnp.bfloat16
    f32 = jnp.float32
    spread = (2, near, far, rows, width)
    vmem = pl.BlockSpec(memory_space=pltpu.VMEM)
    hbm = pl.BlockSpec(memory_space=pl.ANY)
    return pl.pallas_call(
        functools.partial(kernel, far, near),
        out_shape=jax.ShapeDtypeStruct(wavefunction.shape, f32),
        in_specs=[pl.BlockSpec(memory_space=pltpu.SMEM), vmem, hbm, hbm],
        out_specs=vmem,
        scratch_shapes=[
            pltpu.VMEM(left_ops.shape, bf16),
            pltpu.VMEM(right_ops.shape, bf16),
            pltpu.VMEM((nblocks, width, width), bf16),
            pltpu.VMEM((nblocks, width, width), bf16),
            pltpu.VMEM((slots + 1, width, width), f32),
            pltpu.VMEM((2, nblocks, width, width), f32),
            pltpu.VMEM(spread, bf16),
            pltpu.VMEM(spread, bf16),
            pltpu.VMEM(spread, bf16),
            pltpu.VMEM(spread, bf16),
            pltpu.VMEM((2, far, rows, width), bf16),
            pltpu.VMEM((2, far, rows, width), bf16),
            sems((2,)),
            sems((2, 2, far, 2)),
            sems((2, 2, near, far, 2)),
            sems((2, 2, near, far, 2)),
        ],
        compiler_params=pltpu.CompilerParams(
            collective_id=0, has_side_effects=True, vmem_limit_bytes=56 * 1024 * 1024
        ),
        cost_estimate=pl.CostEstimate(
            flops=slots * vectors * 4 * width**3,
            bytes_accessed=4 * left_ops.size,
            transcendentals=0,
        ),
    )(plan, wavefunction, left_ops, right_ops)


def solution(mesh):
    rows = P("grp", "op", None)
    table = P(("grp", "op"), None, None)
    slots = P(("grp", "op"))
    return jax.shard_map(
        functools.partial(per_device, mesh.shape["op"]),
        mesh=mesh,
        in_specs=(rows, table, table, slots, slots, slots, slots, slots),
        out_specs=rows,
        check_vma=False,
    )
```

```python
import functools

import jax
import jax.numpy as jnp
from jax import lax
from jax.experimental import pallas as pl
from jax.experimental.pallas import tpu as pltpu
from jax.sharding import PartitionSpec as P

MESH = pl.DeviceIdType.MESH
UNROLL = 16
SEGMENTS = 6


def plan_terms(raw, live_count, nblocks):
    lanes = raw.shape[1]
    square = (lanes, lanes)
    ids = lax.broadcasted_iota(jnp.int32, (1, lanes), 1)
    across = lax.broadcasted_iota(jnp.int32, square, 1)
    target = jnp.where(ids < live_count, raw[3:4], nblocks)

    def down(row):
        return jnp.broadcast_to(row, square).T

    def count(mask):
        return jnp.sum(mask.astype(jnp.int32), axis=0, keepdims=True)

    key = target * lanes + ids
    rank = down(count(down(key) < key))
    target_down = down(target)

    def sort(values, place):
        return jnp.sum(jnp.where(place, values, 0), axis=0, keepdims=True)

    place = rank == across
    picked = [sort(down(raw[i : i + 1]), place) for i in range(3)]
    ordered = sort(target_down + 1, place)
    before = sort(target_down + 1, rank + 1 == across)
    return picked + [
        (ordered == before).astype(jnp.int32),
        count(target_down <= across),
        (count(target_down == across) > 0).astype(jnp.int32),
    ]


def kernel(far, near, live, left_index, right_index, source_block, target_block, wave, left_hbm, right_hbm, out,
           raw, planned, plan, lefts, rights, psi0, psi1, hist, ended, send_c, recv_c, send_y, recv_y, send_z, recv_z,
           ops_sem, plan_sem, zsem, ysem, csem):
    psi = (psi0, psi1)
    rows = wave.shape[1]
    width = wave.shape[2]
    slots = left_index.shape[1]
    me = lax.axis_index("op")
    c = lax.rem(me, 2)
    y = lax.rem(me // 2, near)
    z = me // (2 * near)

    def index_of(a, b, core):
        return (a * near + b) * 2 + core

    def place_of(idx):
        row = idx * rows
        return row // width, pl.ds(pl.multiple_of(lax.rem(row, width), rows), rows)

    def shift(at, by, size):
        return lax.rem(at + by + size, size)

    sibling = index_of(z, y, 1 - c)
    y_peer = [index_of(z, shift(y, d, near), c) for d in range(near)]
    z_peer = [index_of(shift(z, d, far), y, c) for d in range(far)]
    peers = [sibling] + y_peer[1:] + z_peer[1:]

    loads = [
        pltpu.make_async_copy(left_hbm, lefts, ops_sem.at[0]),
        pltpu.make_async_copy(right_hbm, rights, ops_sem.at[1]),
    ]
    for load in loads:
        load.start()
    barrier = pltpu.get_barrier_semaphore()
    for peer in peers:
        pl.semaphore_signal(barrier, inc=1, device_id={"op": peer}, device_id_type=MESH)
    for v in range(2):
        psi[v][place_of(me)] = wave[v]
    pl.semaphore_wait(barrier, len(peers))

    sent = []

    def remote(src, dst, sems, peer):
        return pltpu.make_async_remote_copy(
            src_ref=src, dst_ref=dst, send_sem=sems[0], recv_sem=sems[1],
            device_id={"op": peer}, device_id_type=MESH,
        )

    def send(src, dst, sems, peer):
        copy = remote(src, dst, sems, peer)
        copy.start()
        sent.append(copy)

    def sem_pair(array, *place):
        return array.at[(*place, 0)], array.at[(*place, 1)]

    def chunk(v, idx):
        return psi[v].at[place_of(idx)]

    def gather_copy(v, sems, idx, peer):
        send(chunk(v, idx), chunk(v, idx), sems, peer)

    def gather_wait(v, sems, idx, peer):
        remote(chunk(v, idx), chunk(v, idx), sems, peer).wait_recv()

    def source(dy, dz, core):
        return index_of(shift(z, -dz, far), shift(y, -dy, near), core)

    def spread(v, dz):
        idx = source(0, dz, c)
        for dy in range(1, near):
            gather_copy(v, sem_pair(ysem, 0, v, dy, dz), idx, y_peer[dy])
        gather_copy(v, sem_pair(csem, 0, v, 0, dz), idx, sibling)

    z_order = sorted(range(1, far), key=lambda d: min(d, far - d))

    def gather_own(v):
        for dz in z_order:
            gather_copy(v, sem_pair(zsem, 0, v, dz), me, z_peer[dz])

    def gather_far(v, order):
        for dz in order:
            gather_wait(v, sem_pair(zsem, 0, v, dz), source(0, dz, c), z_peer[dz])
            spread(v, dz)

    def gather_near(v):
        for dz in [0] + z_order:
            for dy in range(1, near):
                idx = source(dy, dz, c)
                gather_wait(v, sem_pair(ysem, 0, v, dy, dz), idx, y_peer[dy])
                gather_copy(v, sem_pair(csem, 0, v, dy, dz), idx, sibling)

    def gather_end(v):
        for dz in range(far):
            for dy in range(near):
                gather_wait(v, sem_pair(csem, 0, v, dy, dz), source(dy, dz, 1 - c), sibling)

    def terms(v, first, last):
        def body(i, carry):
            base = first + i * UNROLL
            parts = []
            for u in range(UNROLL):
                t = base + u
                block = psi[v][plan[2, t]]
                parts.append(
                    jnp.dot(lefts[plan[0, t]], block, preferred_element_type=jnp.float32)
                    .astype(jnp.bfloat16)
                )
            total = hist[base]
            for u in range(UNROLL):
                t = base + u
                total = total * plan[3, t].astype(jnp.float32) + jnp.dot(
                    parts[u], rights[plan[1, t]], preferred_element_type=jnp.float32
                )
                hist[t + 1] = total
            return carry

        lax.fori_loop(0, (last - first) // UNROLL, body, 0)

    def finish(v):
        for q in range(ended.shape[1]):
            ended[v, q] = hist[plan[4, q]] * plan[5, q].astype(jnp.float32)

    def partial(v, idx):
        return ended[(v, *place_of(idx))]

    f32 = jnp.float32
    bf16 = jnp.bfloat16

    def reduce_core(v):
        finish(v)
        for dy in list(range(1, near)) + [0]:
            for dz in z_order + [0]:
                a, b = shift(z, dz, far), shift(y, dy, near)
                send_c[v, dy, dz] = partial(v, index_of(a, b, 1 - c)).astype(bf16)
                send(send_c.at[v, dy, dz], recv_c.at[v, dy, dz], sem_pair(csem, 1, v, dy, dz), sibling)

    def core_sum(v, dy, dz):
        remote(send_c.at[v, dy, dz], recv_c.at[v, dy, dz], sem_pair(csem, 1, v, dy, dz), sibling).wait_recv()
        a, b = shift(z, dz, far), shift(y, dy, near)
        return partial(v, index_of(a, b, c)) + recv_c[v, dy, dz].astype(f32)

    def reduce_near(v):
        for dz in z_order + [0]:
            for dy in range(1, near):
                send_y[v, dy, dz] = core_sum(v, dy, dz).astype(bf16)
                send(send_y.at[v, dy, dz], recv_y.at[v, dy, dz], sem_pair(ysem, 1, v, dy, dz), y_peer[dy])

    def near_sum(v, dz):
        total = core_sum(v, 0, dz)
        for dy in range(1, near):
            remote(send_y.at[v, dy, dz], recv_y.at[v, dy, dz], sem_pair(ysem, 1, v, dy, dz), y_peer[dy]).wait_recv()
            total = total + recv_y[v, dy, dz].astype(f32)
        return total

    def reduce_far(v, order):
        for dz in order:
            send_z[v, dz] = near_sum(v, dz).astype(bf16)
            send(send_z.at[v, dz], recv_z.at[v, dz], sem_pair(zsem, 1, v, dz), z_peer[dz])

    def reduce_end(v):
        total = near_sum(v, 0)
        for dz in z_order:
            remote(send_z.at[v, dz], recv_z.at[v, dz], sem_pair(zsem, 1, v, dz), z_peer[dz]).wait_recv()
            total = total + recv_z[v, dz].astype(f32)
        out[v] = total

    def segment(v, s):
        cut = [slots * i // (SEGMENTS * UNROLL) * UNROLL for i in (s, s + 1)]
        terms(v, cut[0], slots if s == SEGMENTS - 1 else cut[1])

    first, rest = z_order[:1], z_order[1:]
    spread(0, 0)
    gather_own(0)
    spread(1, 0)
    raw[...] = jnp.zeros_like(raw)
    for row, ref in enumerate((left_index, right_index, source_block, target_block)):
        raw[row : row + 1, 0:slots] = ref[...]
    planned[...] = jnp.zeros_like(planned)
    for row, value in enumerate(plan_terms(raw[...], live[0], psi0.shape[0])):
        planned[row : row + 1, :] = value
    plan_copy = pltpu.make_async_copy(planned, plan, plan_sem)
    plan_copy.start()
    hist[0] = jnp.zeros(hist.shape[1:], f32)
    gather_far(0, z_order)
    gather_own(1)
    gather_near(0)
    gather_far(1, first)
    gather_end(0)
    for load in loads:
        load.wait()
    plan_copy.wait()

    segment(0, 0)
    gather_far(1, rest[: len(rest) // 2])
    segment(0, 1)
    gather_far(1, rest[len(rest) // 2 :])
    for s in range(2, SEGMENTS - 1):
        segment(0, s)
    gather_near(1)
    segment(0, SEGMENTS - 1)
    reduce_core(0)
    gather_end(1)
    segment(1, 0)
    reduce_near(0)
    for s in range(1, SEGMENTS - 1):
        segment(1, s)
    reduce_far(0, first)
    segment(1, SEGMENTS - 1)
    reduce_core(1)
    reduce_far(0, rest)
    reduce_near(1)
    reduce_far(1, z_order)
    reduce_end(0)
    reduce_end(1)
    for copy in sent:
        copy.wait_send()


def per_device(devices, wavefunction, left_ops, right_ops, left_index, right_index,
               source_block, target_block, live_count):
    pairs = devices // 2
    far = 1
    while far * far < pairs:
        far *= 2
    near = pairs // far
    vectors, rows, width = wavefunction.shape
    nblocks = devices * rows // width
    slots = left_index.shape[0]
    lanes = pl.cdiv(slots, 128) * 128
    sems = pltpu.SemaphoreType.DMA
    bf16 = jnp.bfloat16
    f32 = jnp.float32
    spread = (2, near, far, rows, width)
    vmem = pl.BlockSpec(memory_space=pltpu.VMEM)
    hbm = pl.BlockSpec(memory_space=pl.ANY)
    return pl.pallas_call(
        functools.partial(kernel, far, near),
        out_shape=jax.ShapeDtypeStruct(wavefunction.shape, f32),
        in_specs=[pl.BlockSpec(memory_space=pltpu.SMEM)] + [vmem] * 5 + [hbm] * 2,
        out_specs=vmem,
        scratch_shapes=[
            pltpu.VMEM((8, lanes), jnp.int32),
            pltpu.VMEM((8, lanes), jnp.int32),
            pltpu.SMEM((8, lanes), jnp.int32),
            pltpu.VMEM(left_ops.shape, bf16),
            pltpu.VMEM(right_ops.shape, bf16),
            pltpu.VMEM((nblocks, width, width), bf16),
            pltpu.VMEM((nblocks, width, width), bf16),
            pltpu.VMEM((slots + 1, width, width), f32),
            pltpu.VMEM((2, nblocks, width, width), f32),
            pltpu.VMEM(spread, bf16),
            pltpu.VMEM(spread, bf16),
            pltpu.VMEM(spread, bf16),
            pltpu.VMEM(spread, bf16),
            pltpu.VMEM((2, far, rows, width), bf16),
            pltpu.VMEM((2, far, rows, width), bf16),
            sems((2,)),
            sems,
            sems((2, 2, far, 2)),
            sems((2, 2, near, far, 2)),
            sems((2, 2, near, far, 2)),
        ],
        compiler_params=pltpu.CompilerParams(
            collective_id=0, has_side_effects=True, vmem_limit_bytes=56 * 1024 * 1024
        ),
        cost_estimate=pl.CostEstimate(
            flops=slots * vectors * 4 * width**3,
            bytes_accessed=4 * left_ops.size,
            transcendentals=0,
        ),
    )(
        live_count,
        *(x.reshape(1, slots) for x in (left_index, right_index, source_block, target_block)),
        wavefunction,
        left_ops,
        right_ops,
    )


def solution(mesh):
    rows = P("grp", "op", None)
    table = P(("grp", "op"), None, None)
    slots = P(("grp", "op"))
    return jax.shard_map(
        functools.partial(per_device, mesh.shape["op"]),
        mesh=mesh,
        in_specs=(rows, table, table, slots, slots, slots, slots, slots),
        out_specs=rows,
        check_vma=False,
    )
```

```python
import functools

import jax
import jax.numpy as jnp
from jax import lax
from jax.experimental import pallas as pl
from jax.experimental.pallas import tpu as pltpu
from jax.sharding import PartitionSpec as P

MESH = pl.DeviceIdType.MESH
UNROLL = 16
SEGMENTS = 6


def plan_terms(raw, live_count, nblocks):
    lanes = raw.shape[1]
    square = (lanes, lanes)
    ids = lax.broadcasted_iota(jnp.int32, (1, lanes), 1)
    across = lax.broadcasted_iota(jnp.int32, square, 1)
    target = jnp.where(ids < live_count, raw[3:4], nblocks)

    def down(row):
        return jnp.broadcast_to(row, square).T

    def count(mask):
        return jnp.sum(mask.astype(jnp.int32), axis=0, keepdims=True)

    key = target * lanes + ids
    rank = down(count(down(key) < key))
    target_down = down(target)

    def sort(values, place):
        return jnp.sum(jnp.where(place, values, 0), axis=0, keepdims=True)

    place = rank == across
    picked = [sort(down(raw[i : i + 1]), place) for i in range(3)]
    ordered = sort(target_down + 1, place)
    before = sort(target_down + 1, rank + 1 == across)
    return picked + [
        (ordered == before).astype(jnp.int32),
        count(target_down <= across),
        (count(target_down == across) > 0).astype(jnp.int32),
    ]


def kernel(far, near, live, left_index, right_index, source_block, target_block, wave, left_hbm, right_hbm, out,
           raw, planned, plan, lefts, rights, psi0, psi1, hist, ended, send_c, recv_c, send_y, recv_y, send_z, recv_z,
           ops_sem, plan_sem, zsem, ysem, csem):
    psi = (psi0, psi1)
    rows = wave.shape[1]
    width = wave.shape[2]
    slots = left_index.shape[1]
    me = lax.axis_index("op")
    c = lax.rem(me, 2)
    y = lax.rem(me // 2, near)
    z = me // (2 * near)

    def index_of(a, b, core):
        return (a * near + b) * 2 + core

    def place_of(idx):
        row = idx * rows
        return row // width, pl.ds(pl.multiple_of(lax.rem(row, width), rows), rows)

    def shift(at, by, size):
        return lax.rem(at + by + size, size)

    sibling = index_of(z, y, 1 - c)
    y_peer = [index_of(z, shift(y, d, near), c) for d in range(near)]
    z_peer = [index_of(shift(z, d, far), y, c) for d in range(far)]
    peers = [sibling] + y_peer[1:] + z_peer[1:]

    loads = [
        pltpu.make_async_copy(left_hbm, lefts, ops_sem.at[0]),
        pltpu.make_async_copy(right_hbm, rights, ops_sem.at[1]),
    ]
    for load in loads:
        load.start()
    barrier = pltpu.get_barrier_semaphore()
    for peer in peers:
        pl.semaphore_signal(barrier, inc=1, device_id={"op": peer}, device_id_type=MESH)
    for v in range(2):
        psi[v][place_of(me)] = wave[v]
    pl.semaphore_wait(barrier, len(peers))

    sent = []

    def remote(src, dst, sems, peer):
        return pltpu.make_async_remote_copy(
            src_ref=src, dst_ref=dst, send_sem=sems[0], recv_sem=sems[1],
            device_id={"op": peer}, device_id_type=MESH,
        )

    def send(src, dst, sems, peer):
        copy = remote(src, dst, sems, peer)
        copy.start()
        sent.append(copy)

    def sem_pair(array, *place):
        return array.at[(*place, 0)], array.at[(*place, 1)]

    def chunk(v, idx):
        return psi[v].at[place_of(idx)]

    def gather_copy(v, sems, idx, peer):
        send(chunk(v, idx), chunk(v, idx), sems, peer)

    def gather_wait(v, sems, idx, peer):
        remote(chunk(v, idx), chunk(v, idx), sems, peer).wait_recv()

    def source(dy, dz, core):
        return index_of(shift(z, -dz, far), shift(y, -dy, near), core)

    def spread(v, dz):
        idx = source(0, dz, c)
        for dy in range(1, near):
            gather_copy(v, sem_pair(ysem, 0, v, dy, dz), idx, y_peer[dy])
        gather_copy(v, sem_pair(csem, 0, v, 0, dz), idx, sibling)

    z_order = sorted(range(1, far), key=lambda d: min(d, far - d))

    def gather_own(v):
        for dz in z_order:
            gather_copy(v, sem_pair(zsem, 0, v, dz), me, z_peer[dz])

    def gather_far(v, order):
        for dz in order:
            gather_wait(v, sem_pair(zsem, 0, v, dz), source(0, dz, c), z_peer[dz])
            spread(v, dz)

    def gather_near(v):
        for dz in [0] + z_order:
            for dy in range(1, near):
                idx = source(dy, dz, c)
                gather_wait(v, sem_pair(ysem, 0, v, dy, dz), idx, y_peer[dy])
                gather_copy(v, sem_pair(csem, 0, v, dy, dz), idx, sibling)

    def gather_end(v):
        for dz in range(far):
            for dy in range(near):
                gather_wait(v, sem_pair(csem, 0, v, dy, dz), source(dy, dz, 1 - c), sibling)

    def terms(v, first, last):
        def body(i, carry):
            base = first + i * UNROLL
            parts = []
            for u in range(UNROLL):
                t = base + u
                block = psi[v][plan[2, t]]
                parts.append(
                    jnp.dot(lefts[plan[0, t]], block, preferred_element_type=jnp.float32)
                    .astype(jnp.bfloat16)
                )
            total = hist[base]
            for u in range(UNROLL):
                t = base + u
                total = total * plan[3, t].astype(jnp.float32) + jnp.dot(
                    parts[u], rights[plan[1, t]], preferred_element_type=jnp.float32
                )
                hist[t + 1] = total
            return carry

        lax.fori_loop(0, (last - first) // UNROLL, body, 0)

    def finish(v):
        for q in range(ended.shape[1]):
            ended[v, q] = hist[plan[4, q]] * plan[5, q].astype(jnp.float32)

    def partial(v, idx):
        return ended[(v, *place_of(idx))]

    f32 = jnp.float32
    bf16 = jnp.bfloat16

    def reduce_core(v):
        finish(v)
        for dy in list(range(1, near)) + [0]:
            for dz in z_order[::-1] + [0]:
                a, b = shift(z, dz, far), shift(y, dy, near)
                send_c[v, dy, dz] = partial(v, index_of(a, b, 1 - c)).astype(bf16)
                send(send_c.at[v, dy, dz], recv_c.at[v, dy, dz], sem_pair(csem, 1, v, dy, dz), sibling)

    def core_sum(v, dy, dz):
        remote(send_c.at[v, dy, dz], recv_c.at[v, dy, dz], sem_pair(csem, 1, v, dy, dz), sibling).wait_recv()
        a, b = shift(z, dz, far), shift(y, dy, near)
        return partial(v, index_of(a, b, c)) + recv_c[v, dy, dz].astype(f32)

    def reduce_near(v):
        for dz in z_order[::-1] + [0]:
            for dy in range(1, near):
                send_y[v, dy, dz] = core_sum(v, dy, dz).astype(bf16)
                send(send_y.at[v, dy, dz], recv_y.at[v, dy, dz], sem_pair(ysem, 1, v, dy, dz), y_peer[dy])

    def near_sum(v, dz):
        total = core_sum(v, 0, dz)
        for dy in range(1, near):
            remote(send_y.at[v, dy, dz], recv_y.at[v, dy, dz], sem_pair(ysem, 1, v, dy, dz), y_peer[dy]).wait_recv()
            total = total + recv_y[v, dy, dz].astype(f32)
        return total

    def reduce_far(v, order):
        for dz in order[::-1]:
            send_z[v, dz] = near_sum(v, dz).astype(bf16)
            send(send_z.at[v, dz], recv_z.at[v, dz], sem_pair(zsem, 1, v, dz), z_peer[dz])

    def reduce_end(v):
        total = near_sum(v, 0)
        for dz in z_order:
            remote(send_z.at[v, dz], recv_z.at[v, dz], sem_pair(zsem, 1, v, dz), z_peer[dz]).wait_recv()
            total = total + recv_z[v, dz].astype(f32)
        out[v] = total

    def segment(v, s):
        cut = [slots * i // (SEGMENTS * UNROLL) * UNROLL for i in (s, s + 1)]
        terms(v, cut[0], slots if s == SEGMENTS - 1 else cut[1])

    first, rest = z_order[:1], z_order[1:]
    spread(0, 0)
    gather_own(0)
    spread(1, 0)
    raw[...] = jnp.zeros_like(raw)
    for row, ref in enumerate((left_index, right_index, source_block, target_block)):
        raw[row : row + 1, 0:slots] = ref[...]
    planned[...] = jnp.zeros_like(planned)
    for row, value in enumerate(plan_terms(raw[...], live[0], psi0.shape[0])):
        planned[row : row + 1, :] = value
    plan_copy = pltpu.make_async_copy(planned, plan, plan_sem)
    plan_copy.start()
    hist[0] = jnp.zeros(hist.shape[1:], f32)
    gather_far(0, z_order)
    gather_own(1)
    gather_near(0)
    gather_far(1, first)
    gather_end(0)
    for load in loads:
        load.wait()
    plan_copy.wait()

    segment(0, 0)
    gather_far(1, rest[: len(rest) // 2])
    segment(0, 1)
    gather_far(1, rest[len(rest) // 2 :])
    for s in range(2, SEGMENTS - 1):
        segment(0, s)
    gather_near(1)
    segment(0, SEGMENTS - 1)
    reduce_core(0)
    gather_end(1)
    segment(1, 0)
    reduce_near(0)
    for s in range(1, SEGMENTS - 1):
        segment(1, s)
    reduce_far(0, z_order[-1:])
    segment(1, SEGMENTS - 1)
    reduce_core(1)
    reduce_far(0, z_order[:-1])
    reduce_near(1)
    reduce_far(1, z_order)
    reduce_end(0)
    reduce_end(1)
    for copy in sent:
        copy.wait_send()


def per_device(devices, wavefunction, left_ops, right_ops, left_index, right_index,
               source_block, target_block, live_count):
    pairs = devices // 2
    far = 1
    while far * far < pairs:
        far *= 2
    near = pairs // far
    vectors, rows, width = wavefunction.shape
    nblocks = devices * rows // width
    slots = left_index.shape[0]
    lanes = pl.cdiv(slots, 128) * 128
    sems = pltpu.SemaphoreType.DMA
    bf16 = jnp.bfloat16
    f32 = jnp.float32
    spread = (2, near, far, rows, width)
    vmem = pl.BlockSpec(memory_space=pltpu.VMEM)
    hbm = pl.BlockSpec(memory_space=pl.ANY)
    return pl.pallas_call(
        functools.partial(kernel, far, near),
        out_shape=jax.ShapeDtypeStruct(wavefunction.shape, f32),
        in_specs=[pl.BlockSpec(memory_space=pltpu.SMEM)] + [vmem] * 5 + [hbm] * 2,
        out_specs=vmem,
        scratch_shapes=[
            pltpu.VMEM((8, lanes), jnp.int32),
            pltpu.VMEM((8, lanes), jnp.int32),
            pltpu.SMEM((8, lanes), jnp.int32),
            pltpu.VMEM(left_ops.shape, bf16),
            pltpu.VMEM(right_ops.shape, bf16),
            pltpu.VMEM((nblocks, width, width), bf16),
            pltpu.VMEM((nblocks, width, width), bf16),
            pltpu.VMEM((slots + 1, width, width), f32),
            pltpu.VMEM((2, nblocks, width, width), f32),
            pltpu.VMEM(spread, bf16),
            pltpu.VMEM(spread, bf16),
            pltpu.VMEM(spread, bf16),
            pltpu.VMEM(spread, bf16),
            pltpu.VMEM((2, far, rows, width), bf16),
            pltpu.VMEM((2, far, rows, width), bf16),
            sems((2,)),
            sems,
            sems((2, 2, far, 2)),
            sems((2, 2, near, far, 2)),
            sems((2, 2, near, far, 2)),
        ],
        compiler_params=pltpu.CompilerParams(
            collective_id=0, has_side_effects=True, vmem_limit_bytes=56 * 1024 * 1024
        ),
        cost_estimate=pl.CostEstimate(
            flops=slots * vectors * 4 * width**3,
            bytes_accessed=4 * left_ops.size,
            transcendentals=0,
        ),
    )(
        live_count,
        *(x.reshape(1, slots) for x in (left_index, right_index, source_block, target_block)),
        wavefunction,
        left_ops,
        right_ops,
    )


def solution(mesh):
    rows = P("grp", "op", None)
    table = P(("grp", "op"), None, None)
    slots = P(("grp", "op"))
    return jax.shard_map(
        functools.partial(per_device, mesh.shape["op"]),
        mesh=mesh,
        in_specs=(rows, table, table, slots, slots, slots, slots, slots),
        out_specs=rows,
        check_vma=False,
    )
```
